512 devices in a mesh: sec: 64 (over y, z), tp: 8 (over x, core).
Axes of the slice: x: 4, y: 4, z: 16, core: 2. Of those that a mesh axis runs over, the one named last changes fastest.
Arguments:
- ctx_q: bfloat16 [16384, 8192], P('sec', 'tp'), may hold values from -3 to 3
- ctx_kv: bfloat16 [2, 16384, 1024], P(None, 'sec', 'tp'), may hold values from -1000 to 1000
- anchor_kv: bfloat16 [2, 4096, 1024], P(None, 'sec', 'tp'), may hold values from -24 to 24
- counts: int32 [64], P('sec'), may hold values from 64 to 256, as said below
- offsets: int32 [64], P('sec'), may hold values from 0 to 128, as said below
- query_in: bfloat16 [256, 8192], P(None, 'sec'), may hold values from -6 to 6
- w_query: bfloat16 [8192, 8192], P('sec', 'tp'), may hold values from -0.03125 to 0.03125
- w_out: bfloat16 [8192, 8192], P('tp', 'sec'), may hold values from -0.1875 to 0.1875
Outputs:
- ctx_attn: bfloat16 [16384, 8192], P('sec', 'tp')
- result: bfloat16 [256, 8192], P('tp', 'sec')
The draws below stay inside these ranges and needn't reach their ends.
Inputs may be any that keep to these rules, and one draw needn't show every extreme that they name: Each section's first counts[s] tokens are valid; some section is full in every draw. `offsets`: both ends of the range are taken by some section in every draw.
All inputs are finite; a program needn't handle non-finite values.
Results may differ from the reference program's by a relative error of at most 0.02.
The reference program's roundings to bfloat16 on the way count: a program that leaves them out, or rounds other values in their place, can miss the bound.
Values may be sent and summed in bfloat16 or wider, within the bound.
No kernel may reach another device: no remote copies, remote signals or barrier semaphores. Data moves between devices by JAX's collectives and lax.ppermute only.
A program may use at most 192 MiB of HBM per device.

```python
import jax
import jax.numpy as jnp
from jax import lax

D = 8192
H = 64
KVH = 8
HD = 128
SEC_DEV = 256
QSEG = 256
ANCHOR = 4096
SECTIONS = 64
CONTEXT = 16384


def draw_ctx_kv(key, part):
    key = jax.random.fold_in(key, 7)
    subkeys = jax.random.split(key, 1)
    shape = (2, CONTEXT, KVH * HD)
    field = jnp.clip(4.0 * jax.random.normal(subkeys[0], shape, jnp.float32), -24.0, 24.0)
    return field.astype(jnp.bfloat16)


def draw_counts(key, part):
    key = jax.random.fold_in(key, 11)
    subkeys = jax.random.split(key, 2)
    drawn = jax.random.randint(subkeys[0], (SECTIONS,), SEC_DEV // 4, SEC_DEV + 1)
    chosen = jax.random.randint(subkeys[1], (), 0, SECTIONS)
    return jnp.where(jnp.arange(SECTIONS) == chosen, SEC_DEV, drawn).astype(jnp.int32)


def draw_offsets(key, part):
    key = jax.random.fold_in(key, 13)
    subkeys = jax.random.split(key, 3)
    drawn = jax.random.randint(subkeys[0], (SECTIONS,), 0, SEC_DEV // 2 + 1)
    highest = jax.random.randint(subkeys[1], (), 0, SECTIONS)
    lowest = (highest + 1 + jax.random.randint(subkeys[2], (), 0, SECTIONS - 1)) % SECTIONS
    indices = jnp.arange(SECTIONS)
    drawn = jnp.where(indices == highest, SEC_DEV // 2, drawn)
    drawn = jnp.where(indices == lowest, 0, drawn)
    return drawn.astype(jnp.int32)


def block_levels(rng, dims, cuts, low, largest):
    loudness, own = 1.0, jax.random.fold_in(rng, 6)
    for position, shards_of in cuts:
        steps = jnp.exp(jax.random.uniform(jax.random.fold_in(own, position), (shards_of,), jnp.float32, low / len(cuts), largest / len(cuts)))
        loudness = loudness * jnp.repeat(steps, dims[position] // shards_of).reshape([-1 if axis == position else 1 for axis in range(len(dims))])
    return loudness


def bell_draw(rng, dims, scale, limit, cuts=(), kind=jnp.bfloat16):
    values = scale * jax.random.normal(rng, dims, jnp.float32)
    if cuts:
        values = values * block_levels(rng, dims, cuts, -0.22, 0.18)
    return jnp.clip(values, -limit, limit).astype(kind)


def setup_inputs(seed: int = 0) -> dict:
    arg_keys = jax.random.split(jax.random.key(seed), 9)
    return {
        "ctx_q": bell_draw(arg_keys[0], (CONTEXT, H * HD), 0.5, 3.0, ((0, 64), (1, 8))),
        "ctx_kv": draw_ctx_kv(jax.random.fold_in(arg_keys[8], 71), 0),
        "anchor_kv": bell_draw(arg_keys[2], (2, ANCHOR, KVH * HD), 4.0, 24.0, ((1, 64), (2, 8))),
        "counts": draw_counts(jax.random.fold_in(arg_keys[8], 71), 0),
        "offsets": draw_offsets(jax.random.fold_in(arg_keys[8], 71), 0),
        "query_in": bell_draw(arg_keys[5], (QSEG, D), 1.0, 6.0, ((1, 64),)),
        "w_query": bell_draw(arg_keys[6], (D, H * HD), (4 * D) ** -0.5, 0.03125, ((0, 64), (1, 8))),
        "w_out": bell_draw(arg_keys[7], (H * HD, D), (H * HD // 8) ** -0.5, 0.1875, ((0, 8), (1, 64))),
    }


masked_score = -1.0e30


def merge_pair(first, second):
    first_max, first_sum, first_out = first
    second_max, second_sum, second_out = second
    joint_max = jnp.maximum(first_max, second_max)
    first_rate = jnp.exp(first_max - joint_max)
    second_rate = jnp.exp(second_max - joint_max)
    joint_sum = first_sum * first_rate + second_sum * second_rate
    joint_out = first_out * first_rate[..., None] + second_out * second_rate[..., None]
    return (joint_max, joint_sum, joint_out)


def section_partial(queries, key_rows, value_rows, visible):
    scores = jnp.einsum("rgpd,kgd->gprk", queries.astype(jnp.float32), key_rows.astype(jnp.float32)) * HD ** -0.5
    scores = jnp.where(visible, scores, masked_score)
    row_max = scores.max(-1)
    weights = jnp.exp(scores - row_max[..., None])
    row_sum = weights.sum(-1)
    rounded = lax.optimization_barrier(weights.astype(jnp.bfloat16))
    out_sum = jnp.einsum("gprk,kgd->gprd", rounded.astype(jnp.float32), value_rows.astype(jnp.float32))
    return (row_max, row_sum, out_sum)


def reference(ctx_q, ctx_kv, anchor_kv, counts, offsets, query_in, w_query, w_out):
    repeat = H // KVH
    sec_queries = ctx_q.reshape(SECTIONS, SEC_DEV, KVH, repeat, HD)
    sec_keys = ctx_kv[0].reshape(SECTIONS, SEC_DEV, KVH, HD)
    sec_values = ctx_kv[1].reshape(SECTIONS, SEC_DEV, KVH, HD)
    anchor_keys = anchor_kv[0].reshape(ANCHOR, KVH, HD)
    anchor_values = anchor_kv[1].reshape(ANCHOR, KVH, HD)
    positions = jnp.arange(SEC_DEV, dtype=jnp.int32)

    def context_section(operands):
        queries, key_rows, value_rows, valid_len, shift = operands
        own_visible = (positions[None, :] < valid_len) & (positions[None, :] <= positions[:, None] + shift)
        visible = jnp.concatenate([jnp.ones((SEC_DEV, ANCHOR), dtype=bool), own_visible], axis=1)
        all_keys = jnp.concatenate([anchor_keys, key_rows], axis=0)
        all_values = jnp.concatenate([anchor_values, value_rows], axis=0)
        row_max, row_sum, out_sum = section_partial(queries, all_keys, all_values, visible)
        mixed = out_sum / row_sum[..., None]
        return jnp.transpose(mixed, (2, 0, 1, 3)).reshape(SEC_DEV, H * HD).astype(jnp.bfloat16)

    ctx_attn = lax.map(context_section, (sec_queries, sec_keys, sec_values, counts, offsets)).reshape(CONTEXT, H * HD)

    projected = jnp.dot(query_in, w_query, preferred_element_type=jnp.float32).astype(jnp.bfloat16)
    projected = projected.reshape(QSEG, KVH, repeat, HD)

    def query_section(running, operands):
        key_rows, value_rows, valid_len = operands
        visible = positions[None, :] < valid_len
        return merge_pair(running, section_partial(projected, key_rows, value_rows, visible)), None

    start_state = (jnp.full((KVH, repeat, QSEG), masked_score, jnp.float32),
                   jnp.zeros((KVH, repeat, QSEG), jnp.float32),
                   jnp.zeros((KVH, repeat, QSEG, HD), jnp.float32))
    final_state, unused = lax.scan(query_section, start_state, (sec_keys, sec_values, counts))
    row_max, row_sum, out_sum = final_state
    attended = jnp.transpose(out_sum / row_sum[..., None], (2, 0, 1, 3)).reshape(QSEG, H * HD).astype(jnp.bfloat16)
    result = jnp.dot(attended, w_out, preferred_element_type=jnp.float32).astype(jnp.bfloat16)
    return (ctx_attn, result)
```

```python
import functools

import jax
import jax.numpy as jnp
from jax import lax
from jax.experimental import pallas as pl
from jax.experimental.pallas import tpu as pltpu
from jax.sharding import Mesh, PartitionSpec as P

HD = 128
SCALE = HD ** (-0.5)
RATE = SCALE * 1.4426950408889634
masked_score = -1e30
VMEM_LIMIT = 48 * 1024 * 1024


def score_dot(queries, keys):
    return lax.dot_general(
        queries, keys, (((1,), (1,)), ((), ())), preferred_element_type=jnp.float32
    )


def merge_chunk(state, scores, values):
    chunk_max = jnp.max(scores, axis=1, keepdims=True)
    if state is None:
        weights = jnp.exp2((scores - chunk_max) * RATE)
        total = jnp.sum(weights, axis=1, keepdims=True)
        out = jnp.dot(weights.astype(jnp.bfloat16), values, preferred_element_type=jnp.float32)
        return chunk_max, total, out
    row_max, total, out = state
    joint = jnp.maximum(row_max, chunk_max)
    rate = jnp.exp2((row_max - joint) * RATE)
    weights = jnp.exp2((scores - joint) * RATE)
    total = total * rate + jnp.sum(weights, axis=1, keepdims=True)
    part = jnp.dot(weights.astype(jnp.bfloat16), values, preferred_element_type=jnp.float32)
    return joint, total, out * rate + part


def context_kernel(bounds, q_ref, own_ref, anchor_ref, *rest):
    out_ref = rest[-1]
    rows = q_ref.shape[0]
    queries = jnp.concatenate([q_ref[:, :HD], q_ref[:, HD:]], axis=0)
    scores = score_dot(queries, own_ref[0])
    key = lax.broadcasted_iota(jnp.int32, scores.shape, 1)
    row = lax.broadcasted_iota(jnp.int32, scores.shape, 0) & (rows - 1)
    visible = (key < bounds[0]) & (key <= row + bounds[1])
    state = merge_chunk(None, jnp.where(visible, scores, masked_score), own_ref[1])
    for part in range(anchor_ref.shape[0]):
        keys = anchor_ref[part, :, 0].reshape(-1, HD)
        values = anchor_ref[part, :, 1].reshape(-1, HD)
        state = merge_chunk(state, score_dot(queries, keys), values)
    mixed = state[2] / state[1]
    out_ref[:, :HD] = mixed[:rows].astype(jnp.bfloat16)
    out_ref[:, HD:] = mixed[rows:].astype(jnp.bfloat16)


def context_attention(queries, own, anchors, bounds, previous, index):
    rows, width = queries.shape
    columns = pl.BlockSpec((rows, 2 * HD), lambda i, b: (0, index))
    whole = lambda array: pl.BlockSpec(array.shape, lambda i, b: (0,) * array.ndim)
    operands = [queries, own, anchors]
    in_specs = [columns, whole(own), whole(anchors)]
    aliases = {}
    if previous is not None:
        operands.append(previous)
        in_specs.append(pl.BlockSpec(memory_space=pl.ANY))
        aliases = {4: 0}
    keys = own.shape[1] + anchors.size // (2 * HD)
    return pl.pallas_call(
        context_kernel,
        grid_spec=pltpu.PrefetchScalarGridSpec(
            num_scalar_prefetch=1, grid=(1,), in_specs=in_specs, out_specs=columns
        ),
        out_shape=jax.ShapeDtypeStruct((rows, width), jnp.bfloat16),
        input_output_aliases=aliases,
        compiler_params=pltpu.CompilerParams(vmem_limit_bytes=VMEM_LIMIT),
        cost_estimate=pl.CostEstimate(
            flops=16 * rows * keys * HD, bytes_accessed=2 * anchors.size, transcendentals=2 * rows * keys
        ),
    )(bounds, *operands)


def pack_kernel(q_ref, w_ref, out_ref):
    parts, qrows = out_ref.shape[0], q_ref.shape[0]
    depth = w_ref.shape[0]
    heads = w_ref.shape[1] // (parts * HD)
    for part in range(parts):
        out_ref[part, :qrows] = q_ref[...]
        for head in range(heads):
            start = (part * heads + head) * HD
            out_ref[part, qrows + head * depth : qrows + (head + 1) * depth] = w_ref[:, start : start + HD]


def project_kernel(depth, share, in_ref, out_ref):
    nl, rows, width = out_ref.shape
    qrows = nl * rows
    for head in range(width // HD):
        total = 0.0
        for part in range(in_ref.shape[0]):
            start = qrows + head * depth
            total = total + jnp.dot(
                in_ref[part, :qrows],
                in_ref[part, start : start + depth],
                preferred_element_type=jnp.float32,
            )
        for high in range(rows // share):
            for low in range(nl):
                row = (high * nl + low) * share
                out_ref[low, high * share : (high + 1) * share, head * HD : (head + 1) * HD] = total[
                    row : row + share
                ]


def across(row, size):
    return jnp.transpose(jnp.broadcast_to(row, (size, size)))


def section_kernel(length, q_ref, cache_ref, out_ref):
    heads = q_ref.shape[1] // HD
    size = out_ref.shape[1] - 8
    queries = jnp.concatenate([q_ref[:, head * HD : (head + 1) * HD] for head in range(heads)], axis=0)
    state = None
    for first in range(0, cache_ref.shape[0], 4):
        scores, values = [], []
        for part in range(first, first + 4):
            score = score_dot(queries, cache_ref[part, :length])
            values.append(cache_ref[part, length : 2 * length])
            count = cache_ref[part, 2 * length : 2 * length + 16].astype(jnp.float32)
            key = lax.broadcasted_iota(jnp.int32, score.shape, 1).astype(jnp.float32)
            scores.append(jnp.where(key < count[:1, :1], score, masked_score))
        state = merge_chunk(state, jnp.concatenate(scores, axis=1), jnp.concatenate(values, axis=0))
    row_max, total, out = state
    row_max = jnp.transpose(jnp.broadcast_to(row_max, (size, HD)))
    total = jnp.transpose(jnp.broadcast_to(total, (size, HD)))
    stats = jnp.concatenate([row_max[:4], total[:4]], axis=0)
    for copy in range(out_ref.shape[0]):
        out_ref[copy, :size] = out
        out_ref[copy, size:] = stats


def finish_kernel(in_ref, out_ref):
    parts = in_ref.shape[0]
    size = in_ref.shape[1] - 8
    rows = out_ref.shape[1]
    maxes = [in_ref[part, size : size + 1] for part in range(parts)]
    joint = functools.reduce(jnp.maximum, maxes)
    rates = [jnp.exp2((other - joint) * RATE) for other in maxes]
    total = 0.0
    for part in range(parts):
        total = total + rates[part] * in_ref[part, size + 4 : size + 5]
    mixed = 0.0
    for part in range(parts):
        mixed = mixed + across(rates[part], size) * in_ref[part, :size]
    mixed = (mixed / across(total, size)).astype(jnp.bfloat16)
    for copy in range(out_ref.shape[0]):
        for head in range(size // rows):
            out_ref[copy, :, head * HD : (head + 1) * HD] = mixed[head * rows : (head + 1) * rows]


def output_kernel(share, att_ref, w_ref, out_ref):
    ny, nl, each, width = att_ref.shape
    rows = out_ref.shape[1]
    total = 0.0
    for part in range(ny):
        total = total + jnp.dot(
            att_ref[part].reshape(nl * each, width),
            w_ref[part * width : (part + 1) * width],
            preferred_element_type=jnp.float32,
        )
    for low in range(nl):
        for high in range(each // share):
            source = low * each + high * share
            target = (high * nl + low) * share
            offset = target % rows
            out_ref[target // rows, offset : offset + share] = total[source : source + share]


def spread(block, size):
    return jnp.broadcast_to(block[None], (size,) + block.shape)


def solution(mesh):
    ny, nh, nl, nx, nc = 4, 4, 4, 4, 2
    if mesh.shape["sec"] != ny * nh * nl:
        ny, nh, nl, nx, nc = 2, 2, 2, 2, 2
    nz, nt = nh * nl, nx * nc
    fine = Mesh(mesh.devices.reshape(ny, nh, nl, nx, nc), ("y", "h", "l", "x", "c"))
    sec, tp = ("y", "h", "l"), ("x", "c")

    def swap(array, axis):
        return lax.all_to_all(array, axis, 0, 0, tiled=True)

    def double(block, distance):
        pairs = [(z, z ^ distance) for z in range(nz)]
        return jnp.concatenate([block, lax.ppermute(block, ("h", "l"), pairs)], axis=0)

    def body(ctx_q, ctx_kv, anchor_kv, counts, offsets, query_in, w_query, w_out):
        rows = ctx_q.shape[0]
        heads = ctx_q.shape[1] // HD
        qrows, depth = query_in.shape
        part_heads = heads // ny
        width = part_heads * HD
        share = qrows // nz
        bf16, f32 = jnp.bfloat16, jnp.float32
        tie = lax.optimization_barrier

        def kernel(body, shape, dtype, *operands, **kwargs):
            return pl.pallas_call(
                body,
                out_shape=jax.ShapeDtypeStruct(shape, dtype),
                compiler_params=pltpu.CompilerParams(vmem_limit_bytes=VMEM_LIMIT),
                **kwargs,
            )(*operands)

        each = nh * share
        distances = [nz >> (step + 1) for step in range(nz.bit_length() - 1)]
        anchors = anchor_kv[None]

        packed = kernel(pack_kernel, (ny, qrows + part_heads * depth, HD), bf16, query_in, w_query)
        cache = jnp.concatenate(
            [ctx_kv.reshape(2 * rows, HD), jnp.broadcast_to(counts[0].astype(bf16), (16, HD))], axis=0
        )
        packed, cache = tie((packed, cache))
        packed = swap(packed, "y")
        window = [cache[None]]
        for shift in (1, -1, 2)[: nl - 1]:
            pairs = [(z, (z + shift) % nz) for z in range(nz)]
            window.append(lax.ppermute(cache[None], ("h", "l"), pairs))
        packed, window = tie((packed, window))
        caches = lax.all_gather(jnp.concatenate(window, axis=0), "y", axis=0, tiled=True)

        partial = kernel(
            functools.partial(project_kernel, depth, share), (nl, each, width), f32, packed
        )
        partial = swap(partial, "l")
        for distance in distances[:-3]:
            anchors = double(anchors, distance)
        partial, anchors = tie((partial, anchors))
        partial = swap(spread(partial.sum(0), nh), "h")
        for distance in distances[-3:-1]:
            anchors = double(anchors, distance)
        partial, anchors = tie((partial, anchors))
        projected = partial.sum(0).astype(bf16)
        anchors = double(anchors, distances[-1])

        state = kernel(
            functools.partial(section_kernel, rows),
            (nh, part_heads * each + 8, HD),
            f32,
            projected,
            caches,
        )
        state, anchors = tie((state, anchors))
        anchors = lax.all_gather(anchors, "y", axis=0, tiled=False)
        state = swap(state, "h")
        attended = kernel(finish_kernel, (nl, each, width), bf16, state)
        attended = swap(attended, "l")

        bounds = jnp.stack([counts[0], offsets[0]])
        attend = lambda previous, index: context_attention(ctx_q, ctx_kv, anchors, bounds, previous, index)
        attended, anchors = tie((attended, anchors))
        attended = swap(spread(attended, ny), "y")
        ctx_attn = attend(None, 0)
        attended, ctx_attn = tie((attended, ctx_attn))
        product = kernel(
            functools.partial(output_kernel, share), (nt, qrows // nt, HD), f32, attended, w_out
        )
        product, ctx_attn = tie((product, ctx_attn))
        product = swap(product, tp)
        for index in range(1, heads // 2):
            ctx_attn = attend(ctx_attn, index)
        result = product.sum(0).astype(bf16)
        return (ctx_attn, result)

    placed = (
        P(sec, tp),
        P(None, sec, tp),
        P(None, sec, tp),
        P(sec),
        P(sec),
        P(None, sec),
        P(sec, tp),
        P(tp, sec),
    )
    return jax.shard_map(
        body,
        mesh=fine,
        in_specs=placed,
        out_specs=(P(sec, tp), P(tp, sec)),
        check_vma=False,
    )
```

```python
import functools

import jax
import jax.numpy as jnp
from jax import lax
from jax.experimental import pallas as pl
from jax.experimental.pallas import tpu as pltpu
from jax.sharding import Mesh, PartitionSpec as P

HD = 128
SCALE = HD ** (-0.5)
RATE = SCALE * 1.4426950408889634
masked_score = -1e30
VMEM_LIMIT = 48 * 1024 * 1024


def score_dot(queries, keys):
    return lax.dot_general(
        queries, keys, (((1,), (1,)), ((), ())), preferred_element_type=jnp.float32
    )


def merge_chunk(state, scores, values):
    chunk_max = jnp.max(scores, axis=1, keepdims=True)
    if state is None:
        weights = jnp.exp2((scores - chunk_max) * RATE)
        total = jnp.sum(weights, axis=1, keepdims=True)
        out = jnp.dot(weights.astype(jnp.bfloat16), values, preferred_element_type=jnp.float32)
        return chunk_max, total, out
    row_max, total, out = state
    joint = jnp.maximum(row_max, chunk_max)
    rate = jnp.exp2((row_max - joint) * RATE)
    weights = jnp.exp2((scores - joint) * RATE)
    total = total * rate + jnp.sum(weights, axis=1, keepdims=True)
    part = jnp.dot(weights.astype(jnp.bfloat16), values, preferred_element_type=jnp.float32)
    return joint, total, out * rate + part


def context_kernel(bounds, q_ref, own_ref, anchor_ref, *rest):
    out_ref = rest[-1]
    rows = q_ref.shape[0]
    queries = jnp.concatenate([q_ref[:, :HD], q_ref[:, HD:]], axis=0)
    scores = score_dot(queries, own_ref[0])
    key = lax.broadcasted_iota(jnp.int32, scores.shape, 1)
    row = lax.broadcasted_iota(jnp.int32, scores.shape, 0) & (rows - 1)
    visible = (key < bounds[0]) & (key <= row + bounds[1])
    state = merge_chunk(None, jnp.where(visible, scores, masked_score), own_ref[1])
    for part in range(anchor_ref.shape[0]):
        keys = anchor_ref[part, :, 0].reshape(-1, HD)
        values = anchor_ref[part, :, 1].reshape(-1, HD)
        state = merge_chunk(state, score_dot(queries, keys), values)
    mixed = state[2] / state[1]
    out_ref[:, :HD] = mixed[:rows].astype(jnp.bfloat16)
    out_ref[:, HD:] = mixed[rows:].astype(jnp.bfloat16)


def context_attention(queries, own, anchors, bounds, previous, index, steps):
    rows, width = queries.shape
    columns = pl.BlockSpec((rows, 2 * HD), lambda i, b: (0, index + i))
    whole = lambda array: pl.BlockSpec(array.shape, lambda i, b: (0,) * array.ndim)
    operands = [queries, own, anchors]
    in_specs = [columns, whole(own), whole(anchors)]
    aliases = {}
    if previous is not None:
        operands.append(previous)
        in_specs.append(pl.BlockSpec(memory_space=pl.ANY))
        aliases = {4: 0}
    keys = own.shape[1] + anchors.size // (2 * HD)
    return pl.pallas_call(
        context_kernel,
        grid_spec=pltpu.PrefetchScalarGridSpec(
            num_scalar_prefetch=1, grid=(steps,), in_specs=in_specs, out_specs=columns
        ),
        out_shape=jax.ShapeDtypeStruct((rows, width), jnp.bfloat16),
        input_output_aliases=aliases,
        compiler_params=pltpu.CompilerParams(vmem_limit_bytes=VMEM_LIMIT),
        cost_estimate=pl.CostEstimate(
            flops=16 * steps * rows * keys * HD,
            bytes_accessed=2 * anchors.size,
            transcendentals=2 * steps * rows * keys,
        ),
    )(bounds, *operands)


def pack_kernel(q_ref, w_ref, out_ref):
    parts, qrows = out_ref.shape[0], q_ref.shape[0]
    depth = w_ref.shape[0]
    heads = w_ref.shape[1] // (parts * HD)
    for part in range(parts):
        out_ref[part, :qrows] = q_ref[...]
        for head in range(heads):
            start = (part * heads + head) * HD
            out_ref[part, qrows + head * depth : qrows + (head + 1) * depth] = w_ref[:, start : start + HD]


def project_kernel(depth, share, in_ref, out_ref):
    nl, rows, width = out_ref.shape
    qrows = nl * rows
    for head in range(width // HD):
        total = 0.0
        for part in range(in_ref.shape[0]):
            start = qrows + head * depth
            total = total + jnp.dot(
                in_ref[part, :qrows],
                in_ref[part, start : start + depth],
                preferred_element_type=jnp.float32,
            )
        for high in range(rows // share):
            for low in range(nl):
                row = (high * nl + low) * share
                out_ref[low, high * share : (high + 1) * share, head * HD : (head + 1) * HD] = total[
                    row : row + share
                ]


def across(row, size):
    return jnp.transpose(jnp.broadcast_to(row, (size, size)))


def terms(value):
    high = value.astype(jnp.bfloat16).astype(jnp.float32)
    middle = (value - high).astype(jnp.bfloat16).astype(jnp.float32)
    return [high, middle, value - high - middle]


def section_kernel(length, q_ref, cache_ref, out_ref):
    heads = q_ref.shape[1] // HD
    size = out_ref.shape[1] - 16
    queries = jnp.concatenate([q_ref[:, head * HD : (head + 1) * HD] for head in range(heads)], axis=0)
    state = None
    for first in range(0, cache_ref.shape[0], 4):
        scores, values = [], []
        for part in range(first, first + 4):
            score = score_dot(queries, cache_ref[part, :length])
            values.append(cache_ref[part, length : 2 * length])
            count = cache_ref[part, 2 * length : 2 * length + 16].astype(jnp.float32)
            key = lax.broadcasted_iota(jnp.int32, score.shape, 1).astype(jnp.float32)
            scores.append(jnp.where(key < count[:1, :1], score, masked_score))
        state = merge_chunk(state, jnp.concatenate(scores, axis=1), jnp.concatenate(values, axis=0))
    row_max, total, out = state
    row_max = jnp.transpose(jnp.broadcast_to(row_max, (size, HD)))
    total = jnp.transpose(jnp.broadcast_to(total, (size, HD)))
    stats = jnp.concatenate(terms(row_max[:1]) + terms(total[:1]) + [jnp.zeros((10, size), jnp.float32)], axis=0)
    for copy in range(out_ref.shape[0]):
        out_ref[copy, :size] = out.astype(jnp.bfloat16)
        out_ref[copy, size:] = stats.astype(jnp.bfloat16)


def finish_kernel(in_ref, out_ref):
    parts = in_ref.shape[0]
    size = in_ref.shape[1] - 16
    rows = out_ref.shape[1]
    stats = [in_ref[part, size:].astype(jnp.float32) for part in range(parts)]
    maxes = [tile[0:1] + tile[1:2] + tile[2:3] for tile in stats]
    joint = functools.reduce(jnp.maximum, maxes)
    rates = [jnp.exp2((other - joint) * RATE) for other in maxes]
    total, mixed = 0.0, 0.0
    for part in range(parts):
        tile = stats[part]
        total = total + rates[part] * (tile[3:4] + tile[4:5] + tile[5:6])
        mixed = mixed + across(rates[part], size) * in_ref[part, :size].astype(jnp.float32)
    mixed = (mixed / across(total, size)).astype(jnp.bfloat16)
    for copy in range(out_ref.shape[0]):
        for head in range(size // rows):
            out_ref[copy, :, head * HD : (head + 1) * HD] = mixed[head * rows : (head + 1) * rows]


def output_kernel(share, att_ref, w_ref, out_ref):
    ny, nl, each, width = att_ref.shape
    rows = out_ref.shape[1]
    total = 0.0
    for part in range(ny):
        total = total + jnp.dot(
            att_ref[part].reshape(nl * each, width),
            w_ref[part * width : (part + 1) * width],
            preferred_element_type=jnp.float32,
        )
    for low in range(nl):
        for high in range(each // share):
            source = low * each + high * share
            target = (high * nl + low) * share
            offset = target % rows
            out_ref[target // rows, offset : offset + share] = total[source : source + share]


def spread(block, size):
    return jnp.broadcast_to(block[None], (size,) + block.shape)


def solution(mesh):
    ny, nh, nl, nx, nc = 4, 4, 4, 4, 2
    if mesh.shape["sec"] != ny * nh * nl:
        ny, nh, nl, nx, nc = 2, 2, 2, 2, 2
    nz, nt = nh * nl, nx * nc
    fine = Mesh(mesh.devices.reshape(ny, nh, nl, nx, nc), ("y", "h", "l", "x", "c"))
    sec, tp = ("y", "h", "l"), ("x", "c")

    def swap(array, axis):
        return lax.all_to_all(array, axis, 0, 0, tiled=True)

    def body(ctx_q, ctx_kv, anchor_kv, counts, offsets, query_in, w_query, w_out):
        rows = ctx_q.shape[0]
        heads = ctx_q.shape[1] // HD
        qrows, depth = query_in.shape
        part_heads = heads // ny
        width = part_heads * HD
        share = qrows // nz
        bf16, f32 = jnp.bfloat16, jnp.float32
        tie = lax.optimization_barrier

        def kernel(body, shape, dtype, *operands, **kwargs):
            return pl.pallas_call(
                body,
                out_shape=jax.ShapeDtypeStruct(shape, dtype),
                compiler_params=pltpu.CompilerParams(vmem_limit_bytes=VMEM_LIMIT),
                **kwargs,
            )(*operands)

        each = nh * share

        packed = kernel(pack_kernel, (ny, qrows + part_heads * depth, HD), bf16, query_in, w_query)
        cache = jnp.concatenate(
            [ctx_kv.reshape(2 * rows, HD), jnp.broadcast_to(counts[0].astype(bf16), (16, HD))], axis=0
        )
        packed = swap(packed, "y")
        window = [cache[None]]
        for shift in (1, -1, 2)[: nl - 1]:
            pairs = [(z, (z + shift) % nz) for z in range(nz)]
            window.append(lax.ppermute(cache[None], ("h", "l"), pairs))
        packed, window = tie((packed, window))
        caches = lax.all_gather(jnp.concatenate(window, axis=0), "y", axis=0, tiled=True)

        partial = kernel(
            functools.partial(project_kernel, depth, share), (nl, each, width), f32, packed
        )
        partial = swap(partial, "l")
        partial, anchors = tie((spread(partial.sum(0), nh), anchor_kv[None]))
        partial = swap(partial, "h")
        anchors = lax.all_gather(anchors, ("h", "l"), axis=0, tiled=True)
        partial, anchors = tie((partial, anchors))
        projected = partial.sum(0).astype(bf16)

        state = kernel(
            functools.partial(section_kernel, rows),
            (nh, part_heads * each + 16, HD),
            bf16,
            projected,
            caches,
        )
        state, anchors = tie((state, anchors))
        anchors = lax.all_gather(anchors, "y", axis=0, tiled=False)
        state = swap(state, "h")
        attended = kernel(finish_kernel, (nl, each, width), bf16, state)
        attended = swap(attended, "l")

        bounds = jnp.stack([counts[0], offsets[0]])
        attend = lambda previous, index, steps: context_attention(
            ctx_q, ctx_kv, anchors, bounds, previous, index, steps
        )
        attended, anchors = tie((attended, anchors))
        attended = swap(spread(attended, ny), "y")
        ctx_attn = attend(None, 0, 1)
        attended, ctx_attn = tie((attended, ctx_attn))
        product = kernel(
            functools.partial(output_kernel, share), (nt, qrows // nt, HD), f32, attended, w_out
        )
        product, ctx_attn = tie((product, ctx_attn))
        product = swap(product, tp)
        ctx_attn = attend(ctx_attn, 1, heads // 2 - 1)
        result = product.sum(0).astype(bf16)
        return (ctx_attn, result)

    placed = (
        P(sec, tp),
        P(None, sec, tp),
        P(None, sec, tp),
        P(sec),
        P(sec),
        P(None, sec),
        P(sec, tp),
        P(tp, sec),
    )
    return jax.shard_map(
        body,
        mesh=fine,
        in_specs=placed,
        out_specs=(P(sec, tp), P(tp, sec)),
        check_vma=False,
    )
```

```python
import functools

import jax
import jax.numpy as jnp
from jax import lax
from jax.experimental import pallas as pl
from jax.experimental.pallas import tpu as pltpu
from jax.sharding import Mesh, PartitionSpec as P

HD = 128
SCALE = HD ** (-0.5)
RATE = SCALE * 1.4426950408889634
masked_score = -1e30
VMEM_LIMIT = 48 * 1024 * 1024


def score_dot(queries, keys):
    return lax.dot_general(
        queries, keys, (((1,), (1,)), ((), ())), preferred_element_type=jnp.float32
    )


def merge_chunk(state, scores, values):
    chunk_max = jnp.max(scores, axis=1, keepdims=True)
    if state is None:
        weights = jnp.exp2((scores - chunk_max) * RATE)
        total = jnp.sum(weights, axis=1, keepdims=True)
        out = jnp.dot(weights.astype(jnp.bfloat16), values, preferred_element_type=jnp.float32)
        return chunk_max, total, out
    row_max, total, out = state
    joint = jnp.maximum(row_max, chunk_max)
    rate = jnp.exp2((row_max - joint) * RATE)
    weights = jnp.exp2((scores - joint) * RATE)
    total = total * rate + jnp.sum(weights, axis=1, keepdims=True)
    part = jnp.dot(weights.astype(jnp.bfloat16), values, preferred_element_type=jnp.float32)
    return joint, total, out * rate + part


def context_kernel(bounds, q_ref, own_ref, anchor_ref, *rest):
    out_ref = rest[-1]
    rows = q_ref.shape[0]
    queries = jnp.concatenate([q_ref[:, :HD], q_ref[:, HD:]], axis=0)
    scores = score_dot(queries, own_ref[0])
    key = lax.broadcasted_iota(jnp.int32, scores.shape, 1)
    row = lax.broadcasted_iota(jnp.int32, scores.shape, 0) & (rows - 1)
    visible = (key < bounds[0]) & (key <= row + bounds[1])
    state = merge_chunk(None, jnp.where(visible, scores, masked_score), own_ref[1])
    for part in range(anchor_ref.shape[0]):
        keys = anchor_ref[part, :, 0].reshape(-1, HD)
        values = anchor_ref[part, :, 1].reshape(-1, HD)
        state = merge_chunk(state, score_dot(queries, keys), values)
    mixed = state[2] / state[1]
    out_ref[:, :HD] = mixed[:rows].astype(jnp.bfloat16)
    out_ref[:, HD:] = mixed[rows:].astype(jnp.bfloat16)


def context_attention(queries, own, anchors, bounds, previous, index, steps):
    rows, width = queries.shape
    columns = pl.BlockSpec((rows, 2 * HD), lambda i, b: (0, index + i))
    whole = lambda array: pl.BlockSpec(array.shape, lambda i, b: (0,) * array.ndim)
    operands = [queries, own, anchors]
    in_specs = [columns, whole(own), whole(anchors)]
    aliases = {}
    if previous is not None:
        operands.append(previous)
        in_specs.append(pl.BlockSpec(memory_space=pl.ANY))
        aliases = {4: 0}
    keys = own.shape[1] + anchors.size // (2 * HD)
    return pl.pallas_call(
        context_kernel,
        grid_spec=pltpu.PrefetchScalarGridSpec(
            num_scalar_prefetch=1, grid=(steps,), in_specs=in_specs, out_specs=columns
        ),
        out_shape=jax.ShapeDtypeStruct((rows, width), jnp.bfloat16),
        input_output_aliases=aliases,
        compiler_params=pltpu.CompilerParams(vmem_limit_bytes=VMEM_LIMIT),
        cost_estimate=pl.CostEstimate(
            flops=16 * steps * rows * keys * HD,
            bytes_accessed=2 * anchors.size,
            transcendentals=2 * steps * rows * keys,
        ),
    )(bounds, *operands)


def pack_kernel(q_ref, w_ref, out_ref):
    parts, qrows = out_ref.shape[0], q_ref.shape[0]
    depth = w_ref.shape[0]
    heads = w_ref.shape[1] // (parts * HD)
    for part in range(parts):
        out_ref[part, :qrows] = q_ref[...]
        for head in range(heads):
            start = (part * heads + head) * HD
            out_ref[part, qrows + head * depth : qrows + (head + 1) * depth] = w_ref[:, start : start + HD]


def project_kernel(depth, share, in_ref, out_ref):
    nl, rows, width = out_ref.shape
    qrows = nl * rows
    for head in range(width // HD):
        total = 0.0
        for part in range(in_ref.shape[0]):
            start = qrows + head * depth
            total = total + jnp.dot(
                in_ref[part, :qrows],
                in_ref[part, start : start + depth],
                preferred_element_type=jnp.float32,
            )
        for high in range(rows // share):
            for low in range(nl):
                row = (high * nl + low) * share
                out_ref[low, high * share : (high + 1) * share, head * HD : (head + 1) * HD] = total[
                    row : row + share
                ]


def across(row, size):
    return jnp.transpose(jnp.broadcast_to(row, (size, size)))


def terms(value):
    high = value.astype(jnp.bfloat16).astype(jnp.float32)
    middle = (value - high).astype(jnp.bfloat16).astype(jnp.float32)
    return [high, middle, value - high - middle]


def section_kernel(length, q_ref, cache_ref, out_ref):
    heads = q_ref.shape[1] // HD
    size = out_ref.shape[1] - 16
    queries = jnp.concatenate([q_ref[:, head * HD : (head + 1) * HD] for head in range(heads)], axis=0)
    state = None
    for first in range(0, cache_ref.shape[0], 4):
        scores, values = [], []
        for part in range(first, first + 4):
            score = score_dot(queries, cache_ref[part, :length])
            values.append(cache_ref[part, length : 2 * length])
            count = cache_ref[part, 2 * length : 2 * length + 16].astype(jnp.float32)
            key = lax.broadcasted_iota(jnp.int32, score.shape, 1).astype(jnp.float32)
            scores.append(jnp.where(key < count[:1, :1], score, masked_score))
        state = merge_chunk(state, jnp.concatenate(scores, axis=1), jnp.concatenate(values, axis=0))
    row_max, total, out = state
    row_max = jnp.transpose(jnp.broadcast_to(row_max, (size, HD)))
    total = jnp.transpose(jnp.broadcast_to(total, (size, HD)))
    stats = jnp.concatenate(terms(row_max[:1]) + terms(total[:1]) + [jnp.zeros((10, size), jnp.float32)], axis=0)
    for copy in range(out_ref.shape[0]):
        out_ref[copy, :size] = out.astype(jnp.bfloat16)
        out_ref[copy, size:] = stats.astype(jnp.bfloat16)


def finish_kernel(in_ref, out_ref):
    parts = in_ref.shape[0]
    size = in_ref.shape[1] - 16
    rows = out_ref.shape[1]
    stats = [in_ref[part, size:].astype(jnp.float32) for part in range(parts)]
    maxes = [tile[0:1] + tile[1:2] + tile[2:3] for tile in stats]
    joint = functools.reduce(jnp.maximum, maxes)
    rates = [jnp.exp2((other - joint) * RATE) for other in maxes]
    total, mixed = 0.0, 0.0
    for part in range(parts):
        tile = stats[part]
        total = total + rates[part] * (tile[3:4] + tile[4:5] + tile[5:6])
        mixed = mixed + across(rates[part], size) * in_ref[part, :size].astype(jnp.float32)
    mixed = (mixed / across(total, size)).astype(jnp.bfloat16)
    for copy in range(out_ref.shape[0]):
        for head in range(size // rows):
            out_ref[copy, :, head * HD : (head + 1) * HD] = mixed[head * rows : (head + 1) * rows]


def output_kernel(share, att_ref, w_ref, out_ref):
    ny, nl, each, width = att_ref.shape
    rows = out_ref.shape[1]
    total = 0.0
    for part in range(ny):
        total = total + jnp.dot(
            att_ref[part].reshape(nl * each, width),
            w_ref[part * width : (part + 1) * width],
            preferred_element_type=jnp.float32,
        )
    for low in range(nl):
        for high in range(each // share):
            source = low * each + high * share
            target = (high * nl + low) * share
            offset = target % rows
            out_ref[target // rows, offset : offset + share] = total[source : source + share]


def spread(block, size):
    return jnp.broadcast_to(block[None], (size,) + block.shape)


def solution(mesh):
    ny, nh, nl, nx, nc = 4, 4, 4, 4, 2
    if mesh.shape["sec"] != ny * nh * nl:
        ny, nh, nl, nx, nc = 2, 2, 2, 2, 2
    nz, nt = nh * nl, nx * nc
    fine = Mesh(mesh.devices.reshape(ny, nh, nl, nx, nc), ("y", "h", "l", "x", "c"))
    sec, tp = ("y", "h", "l"), ("x", "c")

    def swap(array, axis):
        return lax.all_to_all(array, axis, 0, 0, tiled=True)

    def body(ctx_q, ctx_kv, anchor_kv, counts, offsets, query_in, w_query, w_out):
        rows = ctx_q.shape[0]
        heads = ctx_q.shape[1] // HD
        qrows, depth = query_in.shape
        part_heads = heads // ny
        width = part_heads * HD
        share = qrows // nz
        bf16, f32 = jnp.bfloat16, jnp.float32
        tie = lax.optimization_barrier

        def kernel(body, shape, dtype, *operands, **kwargs):
            return pl.pallas_call(
                body,
                out_shape=jax.ShapeDtypeStruct(shape, dtype),
                compiler_params=pltpu.CompilerParams(vmem_limit_bytes=VMEM_LIMIT),
                **kwargs,
            )(*operands)

        each = nh * share

        packed = kernel(pack_kernel, (ny, qrows + part_heads * depth, HD), bf16, query_in, w_query)
        cache = jnp.concatenate(
            [ctx_kv.reshape(2 * rows, HD), jnp.broadcast_to(counts[0].astype(bf16), (16, HD))], axis=0
        )
        packed = swap(packed, "y")
        window = [cache[None]]
        for shift in (1, -1, 2)[: nl - 1]:
            pairs = [(z, (z + shift) % nz) for z in range(nz)]
            window.append(lax.ppermute(cache[None], ("h", "l"), pairs))
        window, anchors = tie((jnp.concatenate(window, axis=0), anchor_kv[None]))
        caches = lax.all_gather(window, "y", axis=0, tiled=True)
        anchors = lax.all_gather(anchors, ("h", "l"), axis=0, tiled=True)
        packed, anchors = tie((packed, anchors))
        anchors = lax.all_gather(anchors, "y", axis=0, tiled=False)

        partial = kernel(
            functools.partial(project_kernel, depth, share), (nl, each, width), f32, packed
        )
        partial = swap(partial, "l")
        partial = swap(spread(partial.sum(0), nh), "h")
        projected = partial.sum(0).astype(bf16)

        state = kernel(
            functools.partial(section_kernel, rows),
            (nh, part_heads * each + 16, HD),
            bf16,
            projected,
            caches,
        )
        state = swap(state, "h")
        attended = kernel(finish_kernel, (nl, each, width), bf16, state)

        bounds = jnp.stack([counts[0], offsets[0]])
        attend = lambda previous, index, steps: context_attention(
            ctx_q, ctx_kv, anchors, bounds, previous, index, steps
        )
        attended, anchors = tie((attended, anchors))
        attended = swap(attended, "l")
        ctx_attn = attend(None, 0, 1)
        attended, ctx_attn = tie((attended, ctx_attn))
        attended = swap(spread(attended, ny), "y")
        ctx_attn = attend(ctx_attn, 1, 1)
        attended, ctx_attn = tie((attended, ctx_attn))
        product = kernel(
            functools.partial(output_kernel, share), (nt, qrows // nt, HD), f32, attended, w_out
        )
        product, ctx_attn = tie((product, ctx_attn))
        product = swap(product, tp)
        ctx_attn = attend(ctx_attn, 2, heads // 2 - 2)
        result = product.sum(0).astype(bf16)
        return (ctx_attn, result)

    placed = (
        P(sec, tp),
        P(None, sec, tp),
        P(None, sec, tp),
        P(sec),
        P(sec),
        P(None, sec),
        P(sec, tp),
        P(tp, sec),
    )
    return jax.shard_map(
        body,
        mesh=fine,
        in_specs=placed,
        out_specs=(P(sec, tp), P(tp, sec)),
        check_vma=False,
    )
```

```python
import functools

import jax
import jax.numpy as jnp
from jax import lax
from jax.experimental import pallas as pl
from jax.experimental.pallas import tpu as pltpu
from jax.sharding import Mesh, PartitionSpec as P

HD = 128
SCALE = HD ** (-0.5)
RATE = SCALE * 1.4426950408889634
masked_score = -1e30
VMEM_LIMIT = 48 * 1024 * 1024


def score_dot(queries, keys):
    return lax.dot_general(
        queries, keys, (((1,), (1,)), ((), ())), preferred_element_type=jnp.float32
    )


def merge_chunk(state, scores, values):
    chunk_max = jnp.max(scores, axis=1, keepdims=True)
    if state is None:
        weights = jnp.exp2((scores - chunk_max) * RATE)
        total = jnp.sum(weights, axis=1, keepdims=True)
        out = jnp.dot(weights.astype(jnp.bfloat16), values, preferred_element_type=jnp.float32)
        return chunk_max, total, out
    row_max, total, out = state
    joint = jnp.maximum(row_max, chunk_max)
    rate = jnp.exp2((row_max - joint) * RATE)
    weights = jnp.exp2((scores - joint) * RATE)
    total = total * rate + jnp.sum(weights, axis=1, keepdims=True)
    part = jnp.dot(weights.astype(jnp.bfloat16), values, preferred_element_type=jnp.float32)
    return joint, total, out * rate + part


def context_kernel(bounds, q_ref, own_ref, anchor_ref, *rest):
    out_ref = rest[-1]
    rows = q_ref.shape[0]
    queries = jnp.concatenate([q_ref[:, :HD], q_ref[:, HD:]], axis=0)
    scores = score_dot(queries, own_ref[0])
    key = lax.broadcasted_iota(jnp.int32, scores.shape, 1)
    row = lax.broadcasted_iota(jnp.int32, scores.shape, 0) & (rows - 1)
    visible = (key < bounds[0]) & (key <= row + bounds[1])
    state = merge_chunk(None, jnp.where(visible, scores, masked_score), own_ref[1])
    for part in range(anchor_ref.shape[0]):
        keys = anchor_ref[part, :, 0].reshape(-1, HD)
        values = anchor_ref[part, :, 1].reshape(-1, HD)
        state = merge_chunk(state, score_dot(queries, keys), values)
    mixed = state[2] / state[1]
    out_ref[:, :HD] = mixed[:rows].astype(jnp.bfloat16)
    out_ref[:, HD:] = mixed[rows:].astype(jnp.bfloat16)


def context_attention(queries, own, anchors, bounds, previous, index, steps):
    rows, width = queries.shape
    columns = pl.BlockSpec((rows, 2 * HD), lambda i, b: (0, index + i))
    whole = lambda array: pl.BlockSpec(array.shape, lambda i, b: (0,) * array.ndim)
    operands = [queries, own, anchors]
    in_specs = [columns, whole(own), whole(anchors)]
    aliases = {}
    if previous is not None:
        operands.append(previous)
        in_specs.append(pl.BlockSpec(memory_space=pl.ANY))
        aliases = {4: 0}
    keys = own.shape[1] + anchors.size // (2 * HD)
    return pl.pallas_call(
        context_kernel,
        grid_spec=pltpu.PrefetchScalarGridSpec(
            num_scalar_prefetch=1, grid=(steps,), in_specs=in_specs, out_specs=columns
        ),
        out_shape=jax.ShapeDtypeStruct((rows, width), jnp.bfloat16),
        input_output_aliases=aliases,
        compiler_params=pltpu.CompilerParams(vmem_limit_bytes=VMEM_LIMIT),
        cost_estimate=pl.CostEstimate(
            flops=16 * steps * rows * keys * HD,
            bytes_accessed=2 * anchors.size,
            transcendentals=2 * steps * rows * keys,
        ),
    )(bounds, *operands)


def pack_kernel(q_ref, w_ref, out_ref):
    parts, qrows = out_ref.shape[0], q_ref.shape[0]
    depth = w_ref.shape[0]
    heads = w_ref.shape[1] // (parts * HD)
    for part in range(parts):
        out_ref[part, :qrows] = q_ref[...]
        for head in range(heads):
            start = (part * heads + head) * HD
            out_ref[part, qrows + head * depth : qrows + (head + 1) * depth] = w_ref[:, start : start + HD]


def project_kernel(depth, share, in_ref, out_ref):
    nl, rows, width = out_ref.shape
    qrows = nl * rows
    for head in range(width // HD):
        total = 0.0
        for part in range(in_ref.shape[0]):
            start = qrows + head * depth
            total = total + jnp.dot(
                in_ref[part, :qrows],
                in_ref[part, start : start + depth],
                preferred_element_type=jnp.float32,
            )
        for high in range(rows // share):
            for low in range(nl):
                row = (high * nl + low) * share
                out_ref[low, high * share : (high + 1) * share, head * HD : (head + 1) * HD] = total[
                    row : row + share
                ]


def across(row, size):
    return jnp.transpose(jnp.broadcast_to(row, (size, size)))


def terms(value):
    high = value.astype(jnp.bfloat16).astype(jnp.float32)
    middle = (value - high).astype(jnp.bfloat16).astype(jnp.float32)
    return [high, middle, value - high - middle]


def section_kernel(length, q_ref, cache_ref, out_ref):
    heads = q_ref.shape[1] // HD
    size = out_ref.shape[1] - 16
    queries = jnp.concatenate([q_ref[:, head * HD : (head + 1) * HD] for head in range(heads)], axis=0)
    state = None
    for first in range(0, cache_ref.shape[0], 4):
        scores, values = [], []
        for part in range(first, first + 4):
            score = score_dot(queries, cache_ref[part, :length])
            values.append(cache_ref[part, length : 2 * length])
            count = cache_ref[part, 2 * length : 2 * length + 16].astype(jnp.float32)
            key = lax.broadcasted_iota(jnp.int32, score.shape, 1).astype(jnp.float32)
            scores.append(jnp.where(key < count[:1, :1], score, masked_score))
        state = merge_chunk(state, jnp.concatenate(scores, axis=1), jnp.concatenate(values, axis=0))
    row_max, total, out = state
    row_max = jnp.transpose(jnp.broadcast_to(row_max, (size, HD)))
    total = jnp.transpose(jnp.broadcast_to(total, (size, HD)))
    stats = jnp.concatenate(terms(row_max[:1]) + terms(total[:1]) + [jnp.zeros((10, size), jnp.float32)], axis=0)
    for copy in range(out_ref.shape[0]):
        out_ref[copy, :size] = out.astype(jnp.bfloat16)
        out_ref[copy, size:] = stats.astype(jnp.bfloat16)


def finish_kernel(in_ref, out_ref):
    parts = in_ref.shape[0]
    size = in_ref.shape[1] - 16
    rows = out_ref.shape[1]
    stats = [in_ref[part, size:].astype(jnp.float32) for part in range(parts)]
    maxes = [tile[0:1] + tile[1:2] + tile[2:3] for tile in stats]
    joint = functools.reduce(jnp.maximum, maxes)
    rates = [jnp.exp2((other - joint) * RATE) for other in maxes]
    total, mixed = 0.0, 0.0
    for part in range(parts):
        tile = stats[part]
        total = total + rates[part] * (tile[3:4] + tile[4:5] + tile[5:6])
        mixed = mixed + across(rates[part], size) * in_ref[part, :size].astype(jnp.float32)
    mixed = (mixed / across(total, size)).astype(jnp.bfloat16)
    for copy in range(out_ref.shape[0]):
        for head in range(size // rows):
            out_ref[copy, :, head * HD : (head + 1) * HD] = mixed[head * rows : (head + 1) * rows]


def output_kernel(share, att_ref, w_ref, out_ref):
    ny, nl, each, width = att_ref.shape
    rows = out_ref.shape[1]
    total = 0.0
    for part in range(ny):
        total = total + jnp.dot(
            att_ref[part].reshape(nl * each, width),
            w_ref[part * width : (part + 1) * width],
            preferred_element_type=jnp.float32,
        )
    for low in range(nl):
        for high in range(each // share):
            source = low * each + high * share
            target = (high * nl + low) * share
            offset = target % rows
            out_ref[target // rows, offset : offset + share] = total[source : source + share]


def spread(block, size):
    return jnp.broadcast_to(block[None], (size,) + block.shape)


def solution(mesh):
    ny, nh, nl, nx, nc = 4, 4, 4, 4, 2
    if mesh.shape["sec"] != ny * nh * nl:
        ny, nh, nl, nx, nc = 2, 2, 2, 2, 2
    nz, nt = nh * nl, nx * nc
    fine = Mesh(mesh.devices.reshape(ny, nh, nl, nx, nc), ("y", "h", "l", "x", "c"))
    sec, tp = ("y", "h", "l"), ("x", "c")

    def swap(array, axis):
        return lax.all_to_all(array, axis, 0, 0, tiled=True)

    def around(block, step, size):
        got = [block]
        for shift in (step, -step, 2 * step)[: size - 1]:
            pairs = [(z, (z + shift) % nz) for z in range(nz)]
            got.append(lax.ppermute(block, ("h", "l"), pairs))
        return got

    def body(ctx_q, ctx_kv, anchor_kv, counts, offsets, query_in, w_query, w_out):
        rows = ctx_q.shape[0]
        heads = ctx_q.shape[1] // HD
        qrows, depth = query_in.shape
        part_heads = heads // ny
        width = part_heads * HD
        share = qrows // nz
        bf16, f32 = jnp.bfloat16, jnp.float32
        tie = lax.optimization_barrier

        def kernel(body, shape, dtype, *operands, **kwargs):
            return pl.pallas_call(
                body,
                out_shape=jax.ShapeDtypeStruct(shape, dtype),
                compiler_params=pltpu.CompilerParams(vmem_limit_bytes=VMEM_LIMIT),
                **kwargs,
            )(*operands)

        each = nh * share

        packed = kernel(pack_kernel, (ny, qrows + part_heads * depth, HD), bf16, query_in, w_query)
        cache = jnp.concatenate(
            [ctx_kv.reshape(2 * rows, HD), jnp.broadcast_to(counts[0].astype(bf16), (16, HD))], axis=0
        )
        packed = swap(packed, "y")
        packed, window = tie((packed, around(cache[None], 1, nl)))
        caches = lax.all_gather(jnp.concatenate(window, axis=0), "y", axis=0, tiled=True)

        partial = kernel(
            functools.partial(project_kernel, depth, share), (nl, each, width), f32, packed
        )
        partial = swap(partial, "l")
        partial, anchors = tie((partial, around(anchor_kv[None], nl, nh)))
        anchors = jnp.concatenate(anchors, axis=0)
        partial = swap(spread(partial.sum(0), nh), "h")
        partial, anchors = tie((partial, around(anchors, 1, nl)))
        anchors = lax.all_gather(jnp.concatenate(anchors, axis=0), "y", axis=0, tiled=False)
        projected = partial.sum(0).astype(bf16)

        state = kernel(
            functools.partial(section_kernel, rows),
            (nh, part_heads * each + 16, HD),
            bf16,
            projected,
            caches,
        )
        state = swap(state, "h")
        attended = kernel(finish_kernel, (nl, each, width), bf16, state)

        bounds = jnp.stack([counts[0], offsets[0]])
        attend = lambda previous, index, steps: context_attention(
            ctx_q, ctx_kv, anchors, bounds, previous, index, steps
        )
        attended = swap(attended, "l")
        attended = swap(spread(attended, ny), "y")
        product = kernel(
            functools.partial(output_kernel, share), (nt, qrows // nt, HD), f32, attended, w_out
        )
        product, anchors = tie((product, anchors))
        product = swap(product, tp)
        ctx_attn = attend(None, 0, heads // 2)
        result = product.sum(0).astype(bf16)
        return (ctx_attn, result)

    placed = (
        P(sec, tp),
        P(None, sec, tp),
        P(None, sec, tp),
        P(sec),
        P(sec),
        P(None, sec),
        P(sec, tp),
        P(tp, sec),
    )
    return jax.shard_map(
        body,
        mesh=fine,
        in_specs=placed,
        out_specs=(P(sec, tp), P(tp, sec)),
        check_vma=False,
    )
```

```python
import functools

import jax
import jax.numpy as jnp
from jax import lax
from jax.experimental import pallas as pl
from jax.experimental.pallas import tpu as pltpu
from jax.sharding import Mesh, PartitionSpec as P

HD = 128
SCALE = HD ** (-0.5)
RATE = SCALE * 1.4426950408889634
masked_score = -1e30
VMEM_LIMIT = 48 * 1024 * 1024


def score_dot(queries, keys):
    return lax.dot_general(
        queries, keys, (((1,), (1,)), ((), ())), preferred_element_type=jnp.float32
    )


def merge_chunk(state, scores, values):
    chunk_max = jnp.max(scores, axis=1, keepdims=True)
    if state is None:
        weights = jnp.exp2((scores - chunk_max) * RATE)
        total = jnp.sum(weights, axis=1, keepdims=True)
        out = jnp.dot(weights.astype(jnp.bfloat16), values, preferred_element_type=jnp.float32)
        return chunk_max, total, out
    row_max, total, out = state
    joint = jnp.maximum(row_max, chunk_max)
    rate = jnp.exp2((row_max - joint) * RATE)
    weights = jnp.exp2((scores - joint) * RATE)
    total = total * rate + jnp.sum(weights, axis=1, keepdims=True)
    part = jnp.dot(weights.astype(jnp.bfloat16), values, preferred_element_type=jnp.float32)
    return joint, total, out * rate + part


def context_kernel(bounds, q_ref, own_ref, anchor_ref, *rest):
    out_ref = rest[-1]
    rows = q_ref.shape[0]
    queries = jnp.concatenate([q_ref[:, :HD], q_ref[:, HD:]], axis=0)
    scores = score_dot(queries, own_ref[0])
    key = lax.broadcasted_iota(jnp.int32, scores.shape, 1)
    row = lax.broadcasted_iota(jnp.int32, scores.shape, 0) & (rows - 1)
    visible = (key < bounds[0]) & (key <= row + bounds[1])
    state = merge_chunk(None, jnp.where(visible, scores, masked_score), own_ref[1])
    for part in range(anchor_ref.shape[0]):
        keys = anchor_ref[part, :, 0].reshape(-1, HD)
        values = anchor_ref[part, :, 1].reshape(-1, HD)
        state = merge_chunk(state, score_dot(queries, keys), values)
    mixed = state[2] / state[1]
    out_ref[:, :HD] = mixed[:rows].astype(jnp.bfloat16)
    out_ref[:, HD:] = mixed[rows:].astype(jnp.bfloat16)


def context_attention(queries, own, anchors, bounds, previous, index, steps):
    rows, width = queries.shape
    columns = pl.BlockSpec((rows, 2 * HD), lambda i, b: (0, index + i))
    whole = lambda array: pl.BlockSpec(array.shape, lambda i, b: (0,) * array.ndim)
    operands = [queries, own, anchors]
    in_specs = [columns, whole(own), whole(anchors)]
    aliases = {}
    if previous is not None:
        operands.append(previous)
        in_specs.append(pl.BlockSpec(memory_space=pl.ANY))
        aliases = {4: 0}
    keys = own.shape[1] + anchors.size // (2 * HD)
    return pl.pallas_call(
        context_kernel,
        grid_spec=pltpu.PrefetchScalarGridSpec(
            num_scalar_prefetch=1, grid=(steps,), in_specs=in_specs, out_specs=columns
        ),
        out_shape=jax.ShapeDtypeStruct((rows, width), jnp.bfloat16),
        input_output_aliases=aliases,
        compiler_params=pltpu.CompilerParams(vmem_limit_bytes=VMEM_LIMIT),
        cost_estimate=pl.CostEstimate(
            flops=16 * steps * rows * keys * HD,
            bytes_accessed=2 * anchors.size,
            transcendentals=2 * steps * rows * keys,
        ),
    )(bounds, *operands)


def pack_kernel(q_ref, w_ref, out_ref):
    parts, qrows = out_ref.shape[0], q_ref.shape[0]
    depth = w_ref.shape[0]
    heads = w_ref.shape[1] // (parts * HD)
    for part in range(parts):
        out_ref[part, :qrows] = q_ref[...]
        for head in range(heads):
            start = (part * heads + head) * HD
            out_ref[part, qrows + head * depth : qrows + (head + 1) * depth] = w_ref[:, start : start + HD]


def project_kernel(depth, share, in_ref, out_ref):
    nl, rows, width = out_ref.shape
    qrows = nl * rows
    for head in range(width // HD):
        total = 0.0
        for part in range(in_ref.shape[0]):
            start = qrows + head * depth
            total = total + jnp.dot(
                in_ref[part, :qrows],
                in_ref[part, start : start + depth],
                preferred_element_type=jnp.float32,
            )
        for high in range(rows // share):
            for low in range(nl):
                row = (high * nl + low) * share
                out_ref[low, high * share : (high + 1) * share, head * HD : (head + 1) * HD] = total[
                    row : row + share
                ]


def across(row, size):
    return jnp.transpose(jnp.broadcast_to(row, (size, size)))


def terms(value):
    high = value.astype(jnp.bfloat16).astype(jnp.float32)
    middle = (value - high).astype(jnp.bfloat16).astype(jnp.float32)
    return [high, middle, value - high - middle]


def section_kernel(length, q_ref, cache_ref, out_ref):
    heads = q_ref.shape[1] // HD
    size = out_ref.shape[1] - 16
    queries = jnp.concatenate([q_ref[:, head * HD : (head + 1) * HD] for head in range(heads)], axis=0)
    state = None
    for first in range(0, cache_ref.shape[0], 4):
        scores, values = [], []
        for part in range(first, first + 4):
            score = score_dot(queries, cache_ref[part, :length])
            values.append(cache_ref[part, length : 2 * length])
            count = cache_ref[part, 2 * length : 2 * length + 16].astype(jnp.float32)
            key = lax.broadcasted_iota(jnp.int32, score.shape, 1).astype(jnp.float32)
            scores.append(jnp.where(key < count[:1, :1], score, masked_score))
        state = merge_chunk(state, jnp.concatenate(scores, axis=1), jnp.concatenate(values, axis=0))
    row_max, total, out = state
    row_max = jnp.transpose(jnp.broadcast_to(row_max, (size, HD)))
    total = jnp.transpose(jnp.broadcast_to(total, (size, HD)))
    stats = jnp.concatenate(terms(row_max[:1]) + terms(total[:1]) + [jnp.zeros((10, size), jnp.float32)], axis=0)
    for copy in range(out_ref.shape[0]):
        out_ref[copy, :size] = out.astype(jnp.bfloat16)
        out_ref[copy, size:] = stats.astype(jnp.bfloat16)


def finish_kernel(in_ref, out_ref):
    parts = in_ref.shape[0]
    size = in_ref.shape[1] - 16
    rows = out_ref.shape[1]
    stats = [in_ref[part, size:].astype(jnp.float32) for part in range(parts)]
    maxes = [tile[0:1] + tile[1:2] + tile[2:3] for tile in stats]
    joint = functools.reduce(jnp.maximum, maxes)
    rates = [jnp.exp2((other - joint) * RATE) for other in maxes]
    total, mixed = 0.0, 0.0
    for part in range(parts):
        tile = stats[part]
        total = total + rates[part] * (tile[3:4] + tile[4:5] + tile[5:6])
        mixed = mixed + across(rates[part], size) * in_ref[part, :size].astype(jnp.float32)
    mixed = (mixed / across(total, size)).astype(jnp.bfloat16)
    for copy in range(out_ref.shape[0]):
        for head in range(size // rows):
            out_ref[copy, :, head * HD : (head + 1) * HD] = mixed[head * rows : (head + 1) * rows]


def output_kernel(share, att_ref, w_ref, out_ref):
    ny, nl, each, width = att_ref.shape
    rows = out_ref.shape[1]
    total = 0.0
    for part in range(ny):
        total = total + jnp.dot(
            att_ref[part].reshape(nl * each, width),
            w_ref[part * width : (part + 1) * width],
            preferred_element_type=jnp.float32,
        )
    for low in range(nl):
        for high in range(each // share):
            source = low * each + high * share
            target = (high * nl + low) * share
            offset = target % rows
            out_ref[target // rows, offset : offset + share] = total[source : source + share]


def spread(block, size):
    return jnp.broadcast_to(block[None], (size,) + block.shape)


def solution(mesh):
    ny, nh, nl, nx, nc = 4, 4, 4, 4, 2
    if mesh.shape["sec"] != ny * nh * nl:
        ny, nh, nl, nx, nc = 2, 2, 2, 2, 2
    nz, nt = nh * nl, nx * nc
    fine = Mesh(mesh.devices.reshape(ny, nh, nl, nx, nc), ("y", "h", "l", "x", "c"))
    sec, tp = ("y", "h", "l"), ("x", "c")

    def swap(array, axis):
        return lax.all_to_all(array, axis, 0, 0, tiled=True)

    def around(block, step, size):
        got = [block]
        for shift in (step, -step, 2 * step)[: size - 1]:
            pairs = [(z, (z + shift) % nz) for z in range(nz)]
            got.append(lax.ppermute(block, ("h", "l"), pairs))
        return got

    def body(ctx_q, ctx_kv, anchor_kv, counts, offsets, query_in, w_query, w_out):
        rows = ctx_q.shape[0]
        heads = ctx_q.shape[1] // HD
        qrows, depth = query_in.shape
        part_heads = heads // ny
        width = part_heads * HD
        share = qrows // nz
        bf16, f32 = jnp.bfloat16, jnp.float32
        tie = lax.optimization_barrier

        def kernel(body, shape, dtype, *operands, **kwargs):
            return pl.pallas_call(
                body,
                out_shape=jax.ShapeDtypeStruct(shape, dtype),
                compiler_params=pltpu.CompilerParams(vmem_limit_bytes=VMEM_LIMIT),
                **kwargs,
            )(*operands)

        each = nh * share

        packed = kernel(pack_kernel, (ny, qrows + part_heads * depth, HD), bf16, query_in, w_query)
        cache = jnp.concatenate(
            [ctx_kv.reshape(2 * rows, HD), jnp.broadcast_to(counts[0].astype(bf16), (16, HD))], axis=0
        )
        packed = swap(packed, "y")
        packed, window = tie((packed, around(cache[None], 1, nl)))
        caches = lax.all_gather(jnp.concatenate(window, axis=0), "y", axis=0, tiled=True)

        partial = kernel(
            functools.partial(project_kernel, depth, share), (nl, each, width), f32, packed
        )
        partial, anchors = tie((partial, anchor_kv[None]))
        partial = swap(partial, "l")
        anchors = lax.all_gather(anchors, ("h", "l"), axis=0, tiled=True)
        partial, anchors = tie((partial, anchors))
        anchors = lax.all_gather(anchors, "y", axis=0, tiled=False)
        partial = swap(spread(partial.sum(0), nh), "h")
        projected = partial.sum(0).astype(bf16)

        state = kernel(
            functools.partial(section_kernel, rows),
            (nh, part_heads * each + 16, HD),
            bf16,
            projected,
            caches,
        )
        state = swap(state, "h")
        attended = kernel(finish_kernel, (nl, each, width), bf16, state)

        bounds = jnp.stack([counts[0], offsets[0]])
        attend = lambda previous, index, steps: context_attention(
            ctx_q, ctx_kv, anchors, bounds, previous, index, steps
        )
        attended, anchors = tie((attended, anchors))
        attended = swap(attended, "l")
        ctx_attn = attend(None, 0, 1)
        attended, ctx_attn = tie((attended, ctx_attn))
        attended = swap(spread(attended, ny), "y")
        ctx_attn = attend(ctx_attn, 1, 1)
        attended, ctx_attn = tie((attended, ctx_attn))
        product = kernel(
            functools.partial(output_kernel, share), (nt, qrows // nt, HD), f32, attended, w_out
        )
        product, ctx_attn = tie((product, ctx_attn))
        product = swap(product, tp)
        ctx_attn = attend(ctx_attn, 2, heads // 2 - 2)
        result = product.sum(0).astype(bf16)
        return (ctx_attn, result)

    placed = (
        P(sec, tp),
        P(None, sec, tp),
        P(None, sec, tp),
        P(sec),
        P(sec),
        P(None, sec),
        P(sec, tp),
        P(tp, sec),
    )
    return jax.shard_map(
        body,
        mesh=fine,
        in_specs=placed,
        out_specs=(P(sec, tp), P(tp, sec)),
        check_vma=False,
    )
```

```python
import functools

import jax
import jax.numpy as jnp
from jax import lax
from jax.experimental import pallas as pl
from jax.experimental.pallas import tpu as pltpu
from jax.sharding import Mesh, PartitionSpec as P

HD = 128
SCALE = HD ** (-0.5)
RATE = SCALE * 1.4426950408889634
masked_score = -1e30
VMEM_LIMIT = 48 * 1024 * 1024


def score_dot(queries, keys):
    return lax.dot_general(
        queries, keys, (((1,), (1,)), ((), ())), preferred_element_type=jnp.float32
    )


def merge_chunk(state, scores, values):
    chunk_max = jnp.max(scores, axis=1, keepdims=True)
    if state is None:
        weights = jnp.exp2((scores - chunk_max) * RATE)
        total = jnp.sum(weights, axis=1, keepdims=True)
        out = jnp.dot(weights.astype(jnp.bfloat16), values, preferred_element_type=jnp.float32)
        return chunk_max, total, out
    row_max, total, out = state
    joint = jnp.maximum(row_max, chunk_max)
    rate = jnp.exp2((row_max - joint) * RATE)
    weights = jnp.exp2((scores - joint) * RATE)
    total = total * rate + jnp.sum(weights, axis=1, keepdims=True)
    part = jnp.dot(weights.astype(jnp.bfloat16), values, preferred_element_type=jnp.float32)
    return joint, total, out * rate + part


def context_kernel(bounds, q_ref, own_ref, anchor_ref, *rest):
    out_ref = rest[-1]
    rows = q_ref.shape[0]
    queries = jnp.concatenate([q_ref[:, :HD], q_ref[:, HD:]], axis=0)
    scores = score_dot(queries, own_ref[0])
    key = lax.broadcasted_iota(jnp.int32, scores.shape, 1)
    row = lax.broadcasted_iota(jnp.int32, scores.shape, 0) & (rows - 1)
    visible = (key < bounds[0]) & (key <= row + bounds[1])
    state = merge_chunk(None, jnp.where(visible, scores, masked_score), own_ref[1])
    for part in range(anchor_ref.shape[0]):
        keys = anchor_ref[part, :, 0].reshape(-1, HD)
        values = anchor_ref[part, :, 1].reshape(-1, HD)
        state = merge_chunk(state, score_dot(queries, keys), values)
    mixed = state[2] / state[1]
    out_ref[:, :HD] = mixed[:rows].astype(jnp.bfloat16)
    out_ref[:, HD:] = mixed[rows:].astype(jnp.bfloat16)


def context_attention(queries, own, anchors, bounds, previous, index, steps):
    rows, width = queries.shape
    columns = pl.BlockSpec((rows, 2 * HD), lambda i, b: (0, index + i))
    whole = lambda array: pl.BlockSpec(array.shape, lambda i, b: (0,) * array.ndim)
    operands = [queries, own, anchors]
    in_specs = [columns, whole(own), whole(anchors)]
    aliases = {}
    if previous is not None:
        operands.append(previous)
        in_specs.append(pl.BlockSpec(memory_space=pl.ANY))
        aliases = {4: 0}
    keys = own.shape[1] + anchors.size // (2 * HD)
    return pl.pallas_call(
        context_kernel,
        grid_spec=pltpu.PrefetchScalarGridSpec(
            num_scalar_prefetch=1, grid=(steps,), in_specs=in_specs, out_specs=columns
        ),
        out_shape=jax.ShapeDtypeStruct((rows, width), jnp.bfloat16),
        input_output_aliases=aliases,
        compiler_params=pltpu.CompilerParams(vmem_limit_bytes=VMEM_LIMIT),
        cost_estimate=pl.CostEstimate(
            flops=16 * steps * rows * keys * HD,
            bytes_accessed=2 * anchors.size,
            transcendentals=2 * steps * rows * keys,
        ),
    )(bounds, *operands)


def pack_kernel(q_ref, w_ref, out_ref):
    parts, qrows = out_ref.shape[0], q_ref.shape[0]
    depth = w_ref.shape[0]
    heads = w_ref.shape[1] // (parts * HD)
    for part in range(parts):
        out_ref[part, :qrows] = q_ref[...]
        for head in range(heads):
            start = (part * heads + head) * HD
            out_ref[part, qrows + head * depth : qrows + (head + 1) * depth] = w_ref[:, start : start + HD]


def project_kernel(depth, share, in_ref, out_ref):
    nl, rows, width = out_ref.shape
    qrows = nl * rows
    for head in range(width // HD):
        total = 0.0
        for part in range(in_ref.shape[0]):
            start = qrows + head * depth
            total = total + jnp.dot(
                in_ref[part, :qrows],
                in_ref[part, start : start + depth],
                preferred_element_type=jnp.float32,
            )
        for high in range(rows // share):
            for low in range(nl):
                row = (high * nl + low) * share
                out_ref[low, high * share : (high + 1) * share, head * HD : (head + 1) * HD] = total[
                    row : row + share
                ]


def across(row, size):
    return jnp.transpose(jnp.broadcast_to(row, (size, size)))


def terms(value):
    high = value.astype(jnp.bfloat16).astype(jnp.float32)
    middle = (value - high).astype(jnp.bfloat16).astype(jnp.float32)
    return [high, middle, value - high - middle]


def section_kernel(length, q_ref, cache_ref, out_ref):
    heads = q_ref.shape[1] // HD
    size = out_ref.shape[1] - 16
    queries = jnp.concatenate([q_ref[:, head * HD : (head + 1) * HD] for head in range(heads)], axis=0)
    state = None
    for first in range(0, cache_ref.shape[0], 4):
        scores, values = [], []
        for part in range(first, first + 4):
            score = score_dot(queries, cache_ref[part, :length])
            values.append(cache_ref[part, length : 2 * length])
            count = cache_ref[part, 2 * length : 2 * length + 16].astype(jnp.float32)
            key = lax.broadcasted_iota(jnp.int32, score.shape, 1).astype(jnp.float32)
            scores.append(jnp.where(key < count[:1, :1], score, masked_score))
        state = merge_chunk(state, jnp.concatenate(scores, axis=1), jnp.concatenate(values, axis=0))
    row_max, total, out = state
    row_max = jnp.transpose(jnp.broadcast_to(row_max, (size, HD)))
    total = jnp.transpose(jnp.broadcast_to(total, (size, HD)))
    stats = jnp.concatenate(terms(row_max[:1]) + terms(total[:1]) + [jnp.zeros((10, size), jnp.float32)], axis=0)
    for copy in range(out_ref.shape[0]):
        out_ref[copy, :size] = out.astype(jnp.bfloat16)
        out_ref[copy, size:] = stats.astype(jnp.bfloat16)


def finish_kernel(in_ref, out_ref):
    parts = in_ref.shape[0]
    size = in_ref.shape[1] - 16
    rows = out_ref.shape[1]
    stats = [in_ref[part, size:].astype(jnp.float32) for part in range(parts)]
    maxes = [tile[0:1] + tile[1:2] + tile[2:3] for tile in stats]
    joint = functools.reduce(jnp.maximum, maxes)
    rates = [jnp.exp2((other - joint) * RATE) for other in maxes]
    total, mixed = 0.0, 0.0
    for part in range(parts):
        tile = stats[part]
        total = total + rates[part] * (tile[3:4] + tile[4:5] + tile[5:6])
        mixed = mixed + across(rates[part], size) * in_ref[part, :size].astype(jnp.float32)
    mixed = (mixed / across(total, size)).astype(jnp.bfloat16)
    for copy in range(out_ref.shape[0]):
        for head in range(size // rows):
            out_ref[copy, :, head * HD : (head + 1) * HD] = mixed[head * rows : (head + 1) * rows]


def output_kernel(share, att_ref, w_ref, out_ref):
    ny, nl, each, width = att_ref.shape
    rows = out_ref.shape[1]
    total = 0.0
    for part in range(ny):
        total = total + jnp.dot(
            att_ref[part].reshape(nl * each, width),
            w_ref[part * width : (part + 1) * width],
            preferred_element_type=jnp.float32,
        )
    for low in range(nl):
        for high in range(each // share):
            source = low * each + high * share
            target = (high * nl + low) * share
            offset = target % rows
            out_ref[target // rows, offset : offset + share] = total[source : source + share]


def spread(block, size):
    return jnp.broadcast_to(block[None], (size,) + block.shape)


def solution(mesh):
    ny, nh, nl, nx, nc = 4, 4, 4, 4, 2
    if mesh.shape["sec"] != ny * nh * nl:
        ny, nh, nl, nx, nc = 2, 2, 2, 2, 2
    nz, nt = nh * nl, nx * nc
    fine = Mesh(mesh.devices.reshape(ny, nh, nl, nx, nc), ("y", "h", "l", "x", "c"))
    sec, tp = ("y", "h", "l"), ("x", "c")

    def swap(array, axis):
        return lax.all_to_all(array, axis, 0, 0, tiled=True)

    def around(block, step, size):
        got = [block]
        for shift in (step, -step, 2 * step)[: size - 1]:
            pairs = [(z, (z + shift) % nz) for z in range(nz)]
            got.append(lax.ppermute(block, ("h", "l"), pairs))
        return got

    def body(ctx_q, ctx_kv, anchor_kv, counts, offsets, query_in, w_query, w_out):
        rows = ctx_q.shape[0]
        heads = ctx_q.shape[1] // HD
        qrows, depth = query_in.shape
        part_heads = heads // ny
        width = part_heads * HD
        share = qrows // nz
        bf16, f32 = jnp.bfloat16, jnp.float32
        tie = lax.optimization_barrier

        def kernel(body, shape, dtype, *operands, **kwargs):
            return pl.pallas_call(
                body,
                out_shape=jax.ShapeDtypeStruct(shape, dtype),
                compiler_params=pltpu.CompilerParams(vmem_limit_bytes=VMEM_LIMIT),
                **kwargs,
            )(*operands)

        each = nh * share

        packed = kernel(pack_kernel, (ny, qrows + part_heads * depth, HD), bf16, query_in, w_query)
        cache = jnp.concatenate(
            [ctx_kv.reshape(2 * rows, HD), jnp.broadcast_to(counts[0].astype(bf16), (16, HD))], axis=0
        )
        packed = swap(packed, "y")
        packed, window = tie((packed, around(cache[None], 1, nl)))
        caches = lax.all_gather(jnp.concatenate(window, axis=0), "y", axis=0, tiled=True)

        partial = kernel(
            functools.partial(project_kernel, depth, share), (nl, each, width), f32, packed
        )
        partial, anchors = tie((partial, anchor_kv[None]))
        partial = swap(partial, "l")
        anchors = lax.all_gather(anchors, "h", axis=0, tiled=True)
        partial, anchors = tie((partial, anchors))
        partial = swap(spread(partial.sum(0), nh), "h")
        anchors = lax.all_gather(anchors, "l", axis=0, tiled=True)
        partial, anchors = tie((partial, anchors))
        anchors = lax.all_gather(anchors, "y", axis=0, tiled=False)
        projected = partial.sum(0).astype(bf16)

        state = kernel(
            functools.partial(section_kernel, rows),
            (nh, part_heads * each + 16, HD),
            bf16,
            projected,
            caches,
        )
        state = swap(state, "h")
        attended = kernel(finish_kernel, (nl, each, width), bf16, state)

        bounds = jnp.stack([counts[0], offsets[0]])
        attend = lambda previous, index, steps: context_attention(
            ctx_q, ctx_kv, anchors, bounds, previous, index, steps
        )
        attended = swap(attended, "l")
        attended, anchors = tie((attended, anchors))
        attended = swap(spread(attended, ny), "y")
        ctx_attn = attend(None, 0, 1)
        attended, ctx_attn = tie((attended, ctx_attn))
        product = kernel(
            functools.partial(output_kernel, share), (nt, qrows // nt, HD), f32, attended, w_out
        )
        product, ctx_attn = tie((product, ctx_attn))
        product = swap(product, tp)
        ctx_attn = attend(ctx_attn, 1, heads // 2 - 1)
        result = product.sum(0).astype(bf16)
        return (ctx_attn, result)

    placed = (
        P(sec, tp),
        P(None, sec, tp),
        P(None, sec, tp),
        P(sec),
        P(sec),
        P(None, sec),
        P(sec, tp),
        P(tp, sec),
    )
    return jax.shard_map(
        body,
        mesh=fine,
        in_specs=placed,
        out_specs=(P(sec, tp), P(tp, sec)),
        check_vma=False,
    )
```
